32 devices in a mesh: space: 4 (over z), rows: 4 (over y, core), cols: 2 (over x).
Axes of the slice: x: 2, y: 2, z: 4, core: 2. Of those that a mesh axis runs over, the one named last changes fastest.
Arguments:
- occupation: float32 [12288, 2048], P(('cols', 'rows'), 'space'), may hold values from -13.5 to 13.5, as said below
- propagator: float32 [12288, 12288], P('rows', 'cols'), may hold values from -0.5 to 1, as said below
- flags_first: int32 [12288, 2048], P(('cols', 'rows'), 'space'), may hold values from 0 to 2
- flags_second: int32 [12288, 2048], P(('rows', 'cols'), 'space'), may hold values from 0 to 2
- courant: float32 [12288], replicated, may hold values from -0.9 to 0.9
- weights: float32 [12288], replicated, may hold values from 0.5 to 6
Outputs:
- occupation_out: float32 [12288, 2048], P(('cols', 'rows'), 'space')
- temperature: float32 [2048], P('space')
The draws below stay inside these ranges and needn't reach their ends.
Inputs may be any that keep to these rules, and one draw needn't show every extreme that they name: occupation varies from mode to mode and cell to cell. propagator equals its transpose.
All inputs are finite; a program needn't handle non-finite values.
Results may differ from the reference program's by a relative error of at most 0.0003.
Values sent between devices are 32-bit elements; how exact they have to be, the bound alone decides.
A program may use at most 192 MiB of HBM per device.

```python
import math
import jax
import jax.numpy as jnp
from jax import lax

M = 12288
NC = 2048


def draw_occupation(key, part):
    key_scale, key_offset, key_noise = jax.random.split(key, 3)
    scales = jnp.exp(jax.random.uniform(key_scale, (M, 1), jnp.float32, math.log(0.3), math.log(3.0)))
    offsets = jax.random.uniform(key_offset, (1, NC), jnp.float32, -1.5, 1.5)
    noise = jax.random.truncated_normal(key_noise, -4.0, 4.0, (M, NC), jnp.float32)
    return scales * noise + offsets


def draw_propagator(key, part):
    key_off, key_rate = jax.random.split(key, 2)
    raw = jax.random.truncated_normal(key_off, -4.0, 4.0, (M, M), jnp.float32)
    raw = raw * (0.3 / math.sqrt(M))
    symmetric = (raw + raw.T) * (1.0 / math.sqrt(2.0))
    rates = jnp.exp(jax.random.uniform(key_rate, (M,), jnp.float32, math.log(0.5), math.log(5.0)))
    positions = jnp.arange(M)
    return symmetric.at[positions, positions].set(1.0 - 0.15 * rates)


def draw_weights(key, part):
    rising = jnp.exp(math.log(3.0) * jnp.arange(M, dtype=jnp.float32) / M)
    spread = jnp.exp(jax.random.uniform(key, (M,), jnp.float32, math.log(0.5), math.log(2.0)))
    return rising * spread


def touch_ends(array, stream_key, low, top_value):
    place = [jax.random.randint(jax.random.fold_in(stream_key, axis), (), 0, length) for axis, length in enumerate(array.shape)]
    longest = array.shape.index(max(array.shape))
    next_to = place[:longest] + [(place[longest] + 1) % array.shape[longest]] + place[longest + 1:]
    return array.at[tuple(place)].set(low).at[tuple(next_to)].set(top_value)


def setup_inputs(seed: int = 0) -> dict:
    keys = jax.random.split(jax.random.key(seed), 7)
    return {
        "occupation": draw_occupation(jax.random.fold_in(keys[6], 71), 0),
        "propagator": draw_propagator(jax.random.fold_in(keys[6], 71), 0),
        "flags_first": touch_ends(jax.random.randint(keys[2], (M, NC), 0, 3), jax.random.fold_in(keys[2], 1), 0, 2).astype(jnp.int32),
        "flags_second": touch_ends(jax.random.randint(keys[3], (M, NC), 0, 3), jax.random.fold_in(keys[3], 1), 0, 2).astype(jnp.int32),
        "courant": jnp.clip(jax.random.uniform(keys[4], (M,), jnp.float32, -0.9, 0.9), -0.9, 0.9),
        "weights": draw_weights(jax.random.fold_in(keys[6], 71), 0),
    }


highest = lax.Precision.HIGHEST


def limited(left_diff, right_diff, selector):
    left_size = jnp.abs(left_diff)
    right_size = jnp.abs(right_diff)
    agreement = 0.5 * (jnp.sign(left_diff) + jnp.sign(right_diff))
    minmod_size = jnp.minimum(left_size, right_size)
    central_size = jnp.minimum(2.0 * minmod_size, 0.5 * jnp.abs(left_diff + right_diff))
    superbee_size = jnp.maximum(jnp.minimum(2.0 * left_size, right_size), jnp.minimum(left_size, 2.0 * right_size))
    chosen = jnp.where(selector == 0, minmod_size, jnp.where(selector == 1, central_size, superbee_size))
    return agreement * chosen


def advect(padded, selector, courant_col):
    differences = padded[:, 1:] - padded[:, :-1]
    slopes = limited(differences[:, :-1], differences[:, 1:], selector[:, 1:-1])
    centers = padded[:, 1:-1]
    forward = courant_col * (centers[:, :-1] + 0.5 * (1.0 - courant_col) * slopes[:, :-1])
    backward = courant_col * (centers[:, 1:] - 0.5 * (1.0 + courant_col) * slopes[:, 1:])
    fluxes = jnp.where(courant_col > 0.0, forward, backward)
    return padded[:, 2:-2] - (fluxes[:, 1:] - fluxes[:, :-1])


def split_step(field, selector, courant, weights, propagator):
    padded = jnp.pad(field, ((0, 0), (2, 2)))
    padded_flags = jnp.pad(selector, ((0, 0), (2, 2)))
    shifted = advect(padded, padded_flags, courant[:, None])
    heat = jnp.dot(weights, shifted, precision=highest) / jnp.sum(weights)
    deviation = shifted - weights[:, None] * heat[None, :]
    result = jnp.dot(propagator, deviation, precision=highest) + weights[:, None] * heat[None, :]
    return result, heat


def reference(occupation, propagator, flags_first, flags_second, courant, weights):
    middle, heat_first = split_step(occupation, flags_first, courant, weights, propagator)
    final, heat_second = split_step(middle, flags_second, courant, weights, propagator)
    return final, heat_second
```

```python
import jax
import jax.numpy as jnp
from jax import lax
from jax.sharding import PartitionSpec as P

highest = lax.Precision.HIGHEST
high = lax.Precision.HIGH
CHUNKS = (2, 2)


def padded_2(block, sides, width):
    for axis, dim in sides:
        count = lax.axis_size(axis)
        forward = [(i, i + 1) for i in range(count - 1)]
        backward = [(target, source) for source, target in forward]
        low = lax.ppermute(
            lax.slice_in_dim(block, block.shape[dim] - width, None, axis=dim), axis, forward
        )
        high = lax.ppermute(lax.slice_in_dim(block, 0, width, axis=dim), axis, backward)
        block = jnp.concatenate([low, block, high], axis=dim)
    return block


def limited(left_diff, right_diff, selector):
    left_size = jnp.abs(left_diff)
    right_size = jnp.abs(right_diff)
    agreement = 0.5 * (jnp.sign(left_diff) + jnp.sign(right_diff))
    minmod_size = jnp.minimum(left_size, right_size)
    central_size = jnp.minimum(2.0 * minmod_size, 0.5 * jnp.abs(left_diff + right_diff))
    superbee_size = jnp.maximum(
        jnp.minimum(2.0 * left_size, right_size), jnp.minimum(left_size, 2.0 * right_size)
    )
    chosen = jnp.where(
        selector == 0.0, minmod_size, jnp.where(selector == 1.0, central_size, superbee_size)
    )
    return agreement * chosen


def advect(padded, selector, courant_row):
    differences = padded[1:] - padded[:-1]
    slopes = limited(differences[:-1], differences[1:], selector[1:-1])
    centers = padded[1:-1]
    forward = courant_row * (centers[:-1] + 0.5 * (1.0 - courant_row) * slopes[:-1])
    backward = courant_row * (centers[1:] - 0.5 * (1.0 + courant_row) * slopes[1:])
    fluxes = jnp.where(courant_row > 0.0, forward, backward)
    return padded[2:-2] - (fluxes[1:] - fluxes[:-1])


def advect_slab(field, selector_padded, courant_part):
    padded = padded_2(field, (("space", 0),), 2)
    return advect(padded, selector_padded, courant_part[None, :])


def heat_all(weight_part, shifted):
    return lax.psum(jnp.dot(shifted, weight_part, precision=highest), ("rows", "cols"))


def swapped(block, axis, distance):
    count = lax.axis_size(axis)
    return lax.ppermute(block, axis, [(i, i ^ distance) for i in range(count)])


def ordered(bit, mine, other):
    first = bit == 0
    return jnp.concatenate(
        [jnp.where(first, mine, other), jnp.where(first, other, mine)], axis=1
    )


def gathered_rows(block, far):
    if lax.axis_size("rows") != 4:
        return lax.all_gather(block, "rows", axis=1, tiled=True)
    row = lax.axis_index("rows")
    near_pair = ordered(row % 2, block, swapped(block, "rows", 1))
    far_pair = ordered(row % 2, far, swapped(far, "rows", 1))
    return ordered(row // 2, near_pair, far_pair)


def gathered_cols(block):
    if lax.axis_size("cols") != 2:
        return lax.all_gather(block, "cols", axis=1, tiled=True)
    return ordered(lax.axis_index("cols"), block, swapped(block, "cols", 1))


def halves(bit, array):
    width = array.shape[1] // 2
    low, high_part = array[:, :width], array[:, width:]
    first = bit == 0
    return jnp.where(first, low, high_part), jnp.where(first, high_part, low)


def chunks_of(array):
    unit = array.shape[0] // sum(CHUNKS)
    edges = [unit * sum(CHUNKS[:i]) for i in range(len(CHUNKS) + 1)]
    return [array[low:top] for low, top in zip(edges[:-1], edges[1:])]


def after(array, earlier):
    if earlier is None:
        return array
    return lax.optimization_barrier((array, earlier))[0]


def chained_sum(mine, leaving, axis, distance, arrived):
    coming = swapped(after(leaving, arrived), axis, distance)
    return mine + coming, coming


def on_device(occupation, propagator, flags_first, flags_second, courant, weights):
    row_count = lax.axis_size("rows")
    col_count = lax.axis_size("cols")
    row_index = lax.axis_index("rows")
    col_index = lax.axis_index("cols")
    local_modes = occupation.shape[0]
    weight_total = jnp.sum(weights)

    def part(array, block, count):
        return lax.dynamic_slice_in_dim(array, block * count, count)

    offset_first = col_index * row_count + row_index
    offset_second = row_index * col_count + col_index
    weight_first = part(weights, offset_first, local_modes)
    courant_first = part(courant, offset_first, local_modes)
    weight_second = part(weights, offset_second, local_modes)
    courant_second = part(courant, offset_second, local_modes)
    selectors = padded_2(
        jnp.stack([flags_first.T, flags_second.T]).astype(jnp.float32), (("space", 1),), 2
    )

    shifted = advect_slab(occupation.T, selectors[0], courant_first)
    heat = (heat_all(weight_first, shifted) / weight_total)[:, None]
    deviation = shifted - heat * weight_first[None, :]
    pieces = chunks_of(deviation)
    fars = []
    for piece in pieces:
        fars.append(swapped(after(piece, fars[-1] if fars else None), "rows", row_count // 2))
    middles = []
    partial = leaving = arrived = None
    for piece, far in zip(pieces, fars):
        block = after(gathered_rows(piece, after(far, partial)), leaving)
        partial = lax.dot_general(
            block,
            propagator,
            (((1,), (1,)), ((), ())),
            precision=high,
            preferred_element_type=jnp.float32,
        )
        if col_count == 2:
            mine, leaving = halves(col_index, partial)
            total, arrived = chained_sum(mine, leaving, "cols", 1, arrived)
            middles.append(total)
        else:
            middles.append(lax.psum_scatter(partial, "cols", scatter_dimension=1, tiled=True))
    middle = jnp.concatenate(middles, axis=0) + heat * weight_second[None, :]

    shifted_second = advect_slab(middle, selectors[1], courant_second)
    heat_second = heat_all(weight_second, shifted_second) / weight_total
    deviation_second = shifted_second - heat_second[:, None] * weight_second[None, :]
    finals = []
    partial = leaving = arrived = None
    for piece in chunks_of(deviation_second):
        block = after(gathered_cols(piece), leaving)
        partial = lax.dot_general(
            block,
            propagator,
            (((1,), (0,)), ((), ())),
            precision=high,
            preferred_element_type=jnp.float32,
        )
        if row_count == 4:
            near, far = halves(row_index // 2, partial)
            far_mine, far_other = halves(row_index % 2, far)
            near_mine, near_other = halves(row_index % 2, near)
            leaving = far_mine + swapped(far_other, "rows", 1)
            mine = near_mine + swapped(near_other, "rows", 1)
            total, arrived = chained_sum(mine, leaving, "rows", 2, arrived)
            finals.append(total)
        else:
            finals.append(lax.psum_scatter(partial, "rows", scatter_dimension=1, tiled=True))
    final = jnp.concatenate(finals, axis=0) + heat_second[:, None] * weight_first[None, :]
    return (final.T, heat_second)


def solution(mesh):
    placed = (
        P(("cols", "rows"), "space"),
        P("rows", "cols"),
        P(("cols", "rows"), "space"),
        P(("rows", "cols"), "space"),
        P(),
        P(),
    )
    return jax.shard_map(
        on_device,
        mesh=mesh,
        in_specs=placed,
        out_specs=(P(("cols", "rows"), "space"), P("space")),
        check_vma=False,
    )
```
